1024 devices in a mesh: expert: 64 (over x, y, core), mp: 16 (over z).
Axes of the slice: x: 4, y: 8, z: 16, core: 2. Of those that a mesh axis runs over, the one named last changes fastest.
Arguments:
- tokens: bfloat16 [1024, 2048], P('expert', 'mp'), may hold values from -6 to 6
- routes: int32 [1024, 6], P('expert'), may hold values from 0 to 63, all different within a row; in each aligned block of 16 rows (0 to 15, 16 to 31, ...) at most 2 rows name the same one
- probs: float32 [1024, 6], P('expert'), may hold values from 0.1 to 0.6
- w_gate: bfloat16 [64, 2048, 1408], P('expert', None, 'mp'), may hold values from -0.125 to 0.125
- w_up: bfloat16 [64, 2048, 1408], P('expert', None, 'mp'), may hold values from -0.125 to 0.125
- w_down: bfloat16 [64, 1408, 2048], P('expert', 'mp'), may hold values from -0.15625 to 0.15625
- grad_out: bfloat16 [1024, 2048], P('expert', 'mp'), may hold values from -1.5 to 1.5
Outputs:
- mixed: bfloat16 [1024, 2048], P('expert', 'mp')
- grad_tokens: bfloat16 [1024, 2048], P('expert', 'mp')
- grad_probs: float32 [1024, 6], P('expert')
- grad_gate: bfloat16 [64, 2048, 1408], P('expert', None, 'mp')
- grad_up: bfloat16 [64, 2048, 1408], P('expert', None, 'mp')
- grad_down: bfloat16 [64, 1408, 2048], P('expert', 'mp')
The draws below stay inside these ranges and needn't reach their ends.
Inputs may be any that keep to these rules, and one draw needn't show every extreme that they name: `routes`: each row names 6 different experts. In each aligned block of 16 rows (one group) no expert is named by more than 2 rows, and every expert is named by some row.
All inputs are finite; a program needn't handle non-finite values.
Results may differ from the reference program's by a relative error of at most 0.029.
Values may be sent and summed in bfloat16 or wider, within the bound.
A program may use at most 32 MiB of HBM per device.

```python
import math
import jax
import jax.numpy as jnp
import numpy as np
from jax import lax

D = 2048
FF = 1408
TOPK = 6
TOK_DEV = 16
EXPERTS = 64
CAP = 2
FF_BLOCK = 88
TOKENS = 1024
N_EXPERT = 64
N_MP = 16


def block_levels(rng, extent, pieces, low, largest):
    loudness = 1.0
    for position, shards_of in pieces:
        heights = jax.random.uniform(jax.random.fold_in(jax.random.fold_in(rng, 6), position), (shards_of,), jnp.float32, low / len(pieces), largest / len(pieces))
        loudness = loudness * jnp.repeat(jnp.exp(heights), extent[position] // shards_of).reshape((-1,) + (1,) * (len(extent) - 1 - position))
    return loudness


def deal_out(stream_key, own, number, rows, amount, top, most, slope):
    ranking = jax.random.permutation(stream_key, amount)
    packed, ordinary = portions_of(amount, rows * top, most, slope, True), portions_of(amount, rows * top, most, slope, False)
    places = jnp.arange(amount)

    def named(lengths, offset_by):
        used = int((lengths > 0).sum())
        fixed = max(1, used // 4)
        moved = fixed + (places - fixed + offset_by * (used - fixed)) % max(1, amount - fixed)
        return jnp.zeros((amount,), jnp.int32).at[ranking[jnp.where(places < fixed, places, moved)]].set(jnp.asarray(lengths, jnp.int32))

    lengths = jnp.where(number % 4 == 0, named(packed, number // 4), named(ordinary, number - number // 4 - 1))
    mixed = jax.random.permutation(jax.random.fold_in(own, 3), amount)
    giver, receiver = mixed[0:amount // 2 * 2:2], mixed[1:amount // 2 * 2:2]
    slack = jnp.minimum(lengths[giver] - 1, most - lengths[receiver]) // 2
    slack = jnp.where((giver == ranking[0]) | (receiver == ranking[0]) | (lengths[receiver] == 0), 0, jnp.maximum(slack, 0))
    moved = jax.random.randint(jax.random.fold_in(own, 4), (amount // 2,), 0, 1 << 20) % (slack + 1)
    lengths = lengths.at[giver].add(-moved).at[receiver].add(moved)
    labels = jnp.searchsorted(jnp.cumsum(lengths), jnp.arange(rows * top), side="right").astype(jnp.int32)
    table = labels.reshape(top, rows).T
    table = table[jax.random.permutation(jax.random.fold_in(own, 1), rows)]
    offset_by = jax.random.randint(jax.random.fold_in(own, 2), (rows, 1), 0, top)
    return jnp.take_along_axis(table, (jnp.arange(top)[None, :] + offset_by) % top, axis=1)


def portions_of(number_of, total, reach, skew, full):
    loads = [(1 << 20) // math.isqrt(standing ** skew) + 1 for standing in range(1, number_of + 1)]
    largest = reach if full else min(reach, max(-(-total // number_of), total * loads[0] // sum(loads)))
    least = 1 if total - largest >= number_of - 1 else 0
    counts, spare = [largest] + [least] * (number_of - 1), total - largest - least * (number_of - 1)
    while spare > 0:
        candidates = [i for i in range(1, number_of) if counts[i] < largest] or [i for i in range(1, number_of) if counts[i] < reach]
        mass, left = sum([loads[i] for i in candidates]), spare
        for i in candidates:
            addition = min(reach - counts[i], max(1, left * loads[i] // mass), spare)
            counts[i] = counts[i] + addition
            spare = spare - addition
    return np.array(counts)


def centred(key, shape, width, reach, cuts=(), kind=jnp.bfloat16):
    level = block_levels(key, shape, cuts, -0.22, 0.18) if cuts else 1.0
    values = jax.random.normal(key, shape, jnp.float32) * width * level
    return jnp.minimum(jnp.maximum(values, -reach), reach).astype(kind)


def setup_inputs(seed: int = 0) -> dict:
    key_list = jax.random.split(jax.random.key(seed), 8)
    tokens = centred(key_list[0], (TOKENS, D), 1.0, 6.0, ((0, 64), (1, 16)))
    routes_keys = jax.random.split(jax.random.fold_in(key_list[1], 1), TOKENS // TOK_DEV)
    routes_turns = jax.random.permutation(jax.random.fold_in(key_list[1], 3), TOKENS // TOK_DEV)
    routes = jax.vmap(lambda own, number: deal_out(jax.random.fold_in(key_list[1], 2), own, number, TOK_DEV, EXPERTS, TOPK, CAP, 2))(routes_keys, routes_turns).reshape((TOKENS, TOPK))
    probs = jnp.clip(0.1 + 0.5 * jax.random.uniform(key_list[2], (TOKENS, TOPK), jnp.float32) ** block_levels(key_list[2], (TOKENS, TOPK), ((0, 64),), -0.2, 0.2), 0.1, 0.6)
    w_gate = centred(key_list[3], (EXPERTS, D, FF), D ** -0.5, 0.125, ((0, 64), (2, 16)))
    w_up = centred(key_list[4], (EXPERTS, D, FF), D ** -0.5, 0.125, ((0, 64), (2, 16)))
    w_down = centred(key_list[5], (EXPERTS, FF, D), FF ** -0.5, 0.15625, ((0, 64), (1, 16)))
    grad_out = centred(key_list[6], (TOKENS, D), 0.25, 1.5, ((0, 64), (1, 16)))
    return dict(tokens=tokens, routes=routes, probs=probs, w_gate=w_gate, w_up=w_up, w_down=w_down, grad_out=grad_out)


def expert_pass(operands):
    slot_rows, grad_rows, gate_weights, up_weights, down_weights = operands
    highest = lax.Precision.HIGHEST
    rows_in = slot_rows.reshape(-1, D)
    rows_grad = grad_rows.reshape(-1, D)
    row_count = rows_in.shape[0]
    gate_act = jnp.dot(rows_in, gate_weights, preferred_element_type=jnp.float32)
    up_act = jnp.dot(rows_in, up_weights, preferred_element_type=jnp.float32)
    sigmoid_gate = jax.nn.sigmoid(gate_act)
    silu_gate = gate_act * sigmoid_gate
    hidden = (silu_gate * up_act).astype(jnp.bfloat16)
    hidden_blocks = hidden.reshape(row_count, N_MP, FF_BLOCK).astype(jnp.float32)
    down_blocks = down_weights.reshape(N_MP, FF_BLOCK, D).astype(jnp.float32)
    out_block = jnp.einsum("rmf,mfd->mrd", hidden_blocks, down_blocks, precision=highest).astype(jnp.bfloat16)
    expert_out = jnp.sum(out_block.astype(jnp.float32), axis=0).astype(jnp.bfloat16)
    back_hidden = jnp.dot(rows_grad, down_weights.T, preferred_element_type=jnp.float32)
    up_grad = (back_hidden * silu_gate).astype(jnp.bfloat16)
    gate_grad = (back_hidden * up_act * sigmoid_gate * (1.0 + gate_act * (1.0 - sigmoid_gate))).astype(jnp.bfloat16)
    grad_gate = jnp.dot(rows_in.T, gate_grad, preferred_element_type=jnp.float32).astype(jnp.bfloat16)
    grad_up = jnp.dot(rows_in.T, up_grad, preferred_element_type=jnp.float32).astype(jnp.bfloat16)
    grad_down = jnp.dot(hidden.T, rows_grad, preferred_element_type=jnp.float32).astype(jnp.bfloat16)
    gate_blocks = gate_grad.reshape(row_count, N_MP, FF_BLOCK).astype(jnp.float32)
    up_blocks = up_grad.reshape(row_count, N_MP, FF_BLOCK).astype(jnp.float32)
    gate_columns = gate_weights.reshape(D, N_MP, FF_BLOCK).astype(jnp.float32)
    up_columns = up_weights.reshape(D, N_MP, FF_BLOCK).astype(jnp.float32)
    back_block = (jnp.einsum("rmf,dmf->mrd", gate_blocks, gate_columns, precision=highest)
                  + jnp.einsum("rmf,dmf->mrd", up_blocks, up_columns, precision=highest)).astype(jnp.bfloat16)
    slot_back = jnp.sum(back_block.astype(jnp.float32), axis=0).astype(jnp.bfloat16)
    return (expert_out.reshape(slot_rows.shape), slot_back.reshape(slot_rows.shape), grad_gate, grad_up, grad_down)


def reference(tokens, routes, probs, w_gate, w_up, w_down, grad_out):
    highest = lax.Precision.HIGHEST
    token_blocks = tokens.reshape(N_EXPERT, TOK_DEV, D)
    route_blocks = routes.reshape(N_EXPERT, TOK_DEV, TOPK)
    prob_blocks = probs.reshape(N_EXPERT, TOK_DEV, TOPK)
    grad_blocks = grad_out.reshape(N_EXPERT, TOK_DEV, D)
    matches = route_blocks[:, :, :, None] == jnp.arange(EXPERTS, dtype=jnp.int32)[None, None, None, :]
    chosen = jnp.sum(matches.astype(jnp.int32), axis=2)
    weight = jnp.sum(jnp.where(matches, prob_blocks[:, :, :, None], jnp.zeros_like(prob_blocks[:, :, :, None])), axis=2)
    before = jnp.cumsum(chosen, axis=1) - chosen
    slot_ids = jnp.arange(CAP, dtype=jnp.int32)[None, None, None, :]
    one_hot = jnp.where(before[:, :, :, None] == slot_ids, chosen[:, :, :, None], jnp.zeros_like(chosen[:, :, :, None]))
    route_float = one_hot.astype(jnp.float32)
    combine = route_float * weight[:, :, :, None]
    slot_in = jnp.einsum("ngec,ngd->encd", route_float, token_blocks.astype(jnp.float32), precision=highest).astype(jnp.bfloat16)
    slot_grad = jnp.einsum("ngec,ngd->encd", combine, grad_blocks.astype(jnp.float32), precision=highest).astype(jnp.bfloat16)
    expert_out, slot_back, grad_gate, grad_up, grad_down = lax.map(expert_pass, (slot_in, slot_grad, w_gate, w_up, w_down))
    out_float = expert_out.astype(jnp.float32)
    mixed = jnp.einsum("ngec,encd->ngd", combine, out_float, precision=highest).astype(jnp.bfloat16)
    grad_tokens = jnp.einsum("ngec,encd->ngd", route_float, slot_back.astype(jnp.float32), precision=highest).astype(jnp.bfloat16)
    scores = jnp.einsum("encd,ngd->ngec", out_float, grad_blocks.astype(jnp.float32), precision=highest)
    per_expert = jnp.sum(route_float * scores, axis=3)
    grad_probs = jnp.sum(jnp.where(matches, per_expert[:, :, None, :], jnp.zeros_like(per_expert[:, :, None, :])), axis=3)
    return (mixed.reshape(TOKENS, D), grad_tokens.reshape(TOKENS, D), grad_probs.reshape(TOKENS, TOPK), grad_gate, grad_up, grad_down)
```

```python
import functools

import jax
import jax.numpy as jnp
from jax import lax
from jax.experimental import pallas as pl
from jax.experimental.pallas import tpu as pltpu
from jax.sharding import PartitionSpec as P

MESH = pl.DeviceIdType.MESH
BF = jnp.bfloat16
F32 = jnp.float32


def dot(a, b):
    return jnp.dot(a, b, preferred_element_type=F32)


def dot_nt(a, b):
    return lax.dot_general(a, b, (((1,), (1,)), ((), ())), preferred_element_type=F32)


def kernel(
    ny, nxc, nz,
    tok, gout, rt, pt, wg_h, wu_h, wd_h,
    mixed, gtok, gprob, ogg, ogu, ogd,
    wg, wu, wd, disp, disp_t, s_buf, r1, b_buf, xg, acc, h_t, h_r, part, tx, rx, own,
    sc_own, sc_all, o_buf, q1, q2, home, gw,
    w_sem, ow_sem, a1_send, a1_recv, a2_send, a2_recv, ag_send, ag_recv, rs_send, rs_recv,
    sc_send, sc_recv, b1_send, b1_recv, b2_send, b2_recv,
):
    e = lax.axis_index("expert")
    m = lax.axis_index("mp")
    x_me = e // (2 * ny)
    y_me = (e // 2) % ny
    xc_me = x_me * 2 + e % 2
    half = nz // 2
    rows = ny * nxc * 2
    nt = tok.shape[0]
    topk = rt.shape[0]

    def y_peer(d):
        y2 = lax.rem(y_me + d, ny)
        return y2, (x_me * ny + y2) * 2 + e % 2

    def xc_peer(d):
        xc2 = lax.rem(xc_me + d, nxc)
        return xc2, ((xc2 // 2) * ny + y_me) * 2 + xc2 % 2

    def z_at(d):
        return lax.rem(m + d + 2 * nz, nz)

    right, left = z_at(1), z_at(-1)

    loads = [
        pltpu.make_async_copy(src, dst, w_sem.at[i])
        for i, (src, dst) in enumerate(((wg_h, wg), (wu_h, wu), (wd_h, wd)))
    ]
    for c in loads:
        c.start()

    barrier = pltpu.get_barrier_semaphore()
    for d in range(1, ny):
        pl.semaphore_signal(barrier, inc=1, device_id={"expert": y_peer(d)[1]}, device_id_type=MESH)
    for d in range(1, nxc):
        pl.semaphore_signal(barrier, inc=1, device_id={"expert": xc_peer(d)[1]}, device_id_type=MESH)
    for d in range(1, nz):
        pl.semaphore_signal(barrier, inc=1, device_id={"mp": z_at(d)}, device_id_type=MESH)

    r = lax.broadcasted_iota(jnp.int32, (rows, nt), 0)
    sy = nxc * 2
    y_r = r // sy
    xc_r = (r % sy) // 2
    slot_r = r % 2
    e_r = (xc_r // 2) * (2 * ny) + y_r * 2 + xc_r % 2
    chosen = jnp.zeros((rows, nt), F32)
    weight = jnp.zeros((rows, nt), F32)
    for k in range(topk):
        hit = rt[k : k + 1, :] == e_r
        chosen = jnp.where(hit, 1.0, chosen)
        weight = jnp.where(hit, pt[k : k + 1, :], weight)
    t0 = lax.broadcasted_iota(jnp.int32, (nt, nt), 0)
    t1 = lax.broadcasted_iota(jnp.int32, (nt, nt), 1)
    earlier = jnp.where(t0 < t1, 1.0, 0.0).astype(BF)
    before = dot(chosen.astype(BF), earlier)
    d_f = jnp.where(before == slot_r.astype(F32), chosen, 0.0)
    d_w = d_f * weight
    disp[...] = d_f
    d_b = d_f.astype(BF)
    w_row = jnp.sum(d_w, axis=1, keepdims=True)
    s_buf[0] = dot(d_b, tok[...]).astype(BF)
    s_buf[1] = (dot(d_b, gout[...]) * w_row).astype(BF)

    pl.semaphore_wait(barrier, (ny - 1) + (nxc - 1) + (nz - 1))

    def chunk(i, n):
        return pl.ds(pl.multiple_of(i * n, n), n)

    def send_y(src, dst, ss, rs):
        copies = []
        for d in range(1, ny):
            y2, peer = y_peer(d)
            c = pltpu.make_async_remote_copy(
                src_ref=src.at[:, chunk(y2, sy), :], dst_ref=dst.at[:, chunk(y_me, sy), :],
                send_sem=ss.at[d], recv_sem=rs.at[d], device_id={"expert": peer}, device_id_type=MESH)
            c.start()
            copies.append(c)
        dst[:, chunk(y_me, sy), :] = src[:, chunk(y_me, sy), :]
        return copies

    sx = ny * 2

    def send_xc(src, dst, ss, rs):
        copies = []
        for d in range(1, nxc):
            xc2, peer = xc_peer(d)
            c = pltpu.make_async_remote_copy(
                src_ref=src.at[:, chunk(xc2, sx), :], dst_ref=dst.at[:, chunk(xc_me, sx), :],
                send_sem=ss.at[d], recv_sem=rs.at[d], device_id={"expert": peer}, device_id_type=MESH)
            c.start()
            copies.append(c)
        dst[:, chunk(xc_me, sx), :] = src[:, chunk(xc_me, sx), :]
        return copies

    pending = []

    a1 = send_y(s_buf, r1, a1_send, a1_recv)
    pending += a1

    t_f = jnp.transpose(d_f)
    t_w = jnp.transpose(d_w)
    t_hi = t_w.astype(BF)
    disp_t[0] = t_hi
    disp_t[1] = (t_w - t_hi.astype(F32)).astype(BF)
    disp_t[2] = t_f.astype(BF)
    p0 = lax.broadcasted_iota(jnp.int32, (rows, rows), 0)
    p1 = lax.broadcasted_iota(jnp.int32, (rows, rows), 1)
    source = ((p0 % sx) // 2) * sy + (p0 // sx) * 2 + p0 % 2
    swap = jnp.where(p1 == source, 1.0, 0.0).astype(BF)
    for a in range(3):
        acc[a] = jnp.zeros(acc.shape[1:], F32)

    for c in a1:
        c.wait_recv()
    for a in range(2):
        b_buf[a] = dot(swap, r1[a]).astype(BF)

    a2 = send_xc(b_buf, xg.at[m], a2_send, a2_recv)
    pending += a2
    for c in loads:
        c.wait()
    for c in a2:
        c.wait_recv()

    def hop(way, a, s):
        to, sign = ((right, -1), (left, 1))[way]
        blk = z_at(sign * (s - 1))
        return pltpu.make_async_remote_copy(
            src_ref=xg.at[blk, a], dst_ref=xg.at[blk, a],
            send_sem=ag_send.at[way, a, s], recv_sem=ag_recv.at[way, a, s],
            device_id={"mp": to}, device_id_type=MESH)

    def cols(blk):
        return pl.ds(pl.multiple_of(blk * 128, 128), 128)

    def use(blk, a):
        v = xg[blk, a]
        if a == 0:
            acc[0] += dot_nt(wg[:, cols(blk)], v)
            acc[1] += dot_nt(wu[:, cols(blk)], v)
        else:
            acc[2] += dot_nt(wd[:, cols(blk)], v)

    def last(way, a):
        return half if way == a else half - 1

    for a in range(2):
        for way in range(2):
            hop(way, a, 1).start()
    for a in range(2):
        use(m, a)

    def ag_step(s, full):
        for a in range(2):
            for way in range(2):
                hop(way, a, s).wait_recv()
                if full or s < last(way, a):
                    hop(way, a, s + 1).start()
        for a in range(2):
            for way in range(2):
                use(z_at((-1, 1)[way] * s), a)

    def ag_body(s, carry):
        ag_step(s, True)
        return carry

    lax.fori_loop(1, half - 1, ag_body, 0)
    ag_step(half - 1, False)
    for a in range(2):
        hop(a, a, half).wait_recv()
    for a in range(2):
        use(z_at(half), a)

    gate, up, back = acc[0], acc[1], acc[2]
    sig = jax.nn.sigmoid(gate)
    silu = gate * sig
    hid = silu * up
    u_g = back * silu
    g_g = back * up * sig * (1.0 + gate * (1.0 - sig))
    sc_own[...] = jnp.broadcast_to(jnp.sum(hid * back, axis=0, keepdims=True), sc_own.shape)
    scores = []
    for d in range(1, nz):
        c = pltpu.make_async_remote_copy(
            src_ref=sc_own, dst_ref=sc_all.at[m], send_sem=sc_send.at[d], recv_sem=sc_recv.at[d],
            device_id={"mp": z_at(d)}, device_id_type=MESH)
        c.start()
        scores.append(c)
    pending += scores
    for i, v in enumerate((hid, g_g, u_g)):
        h_r[i] = jnp.transpose(v).astype(BF)
        h_t[i] = v.astype(BF)

    def blk_at(way, a, s):
        n = last(way, a)
        return z_at(n + 1 - s) if way == 0 else z_at(s - n - 1)

    def partial(a, blk):
        if a == 0:
            return dot(h_r[0], wd[:, cols(blk)])
        return dot(h_r[1], wg[:, cols(blk)]) + dot(h_r[2], wu[:, cols(blk)])

    def turn(way, a, s):
        return pltpu.make_async_remote_copy(
            src_ref=tx.at[way, a, s], dst_ref=rx.at[way, a, s],
            send_sem=rs_send.at[way, a, s], recv_sem=rs_recv.at[way, a, s],
            device_id={"mp": (right, left)[way]}, device_id_type=MESH)

    def weights_of(blk):
        x_v, g_v = xg[blk, 0], xg[blk, 1]
        gw[0, :, cols(blk)] = dot(h_t[1], x_v).astype(BF)
        gw[1, :, cols(blk)] = dot(h_t[2], x_v).astype(BF)
        gw[2, :, cols(blk)] = dot(h_t[0], g_v).astype(BF)

    for a in range(2):
        for way in range(2):
            tx[way, a, 1] = partial(a, blk_at(way, a, 1)).astype(BF)
            turn(way, a, 1).start()
    for a in range(2):
        for way in range(2):
            part[way, a] = partial(a, blk_at(way, a, 2))
    weights_of(0)
    weights_of(1)

    def rs_step(s, full):
        for a in range(2):
            for way in range(2):
                if full or s <= last(way, a):
                    turn(way, a, s - 1).wait_recv()
                    tx[way, a, s] = (part[way, a] + rx[way, a, s - 1].astype(F32)).astype(BF)
                    turn(way, a, s).start()
        for a in range(2):
            for way in range(2):
                if full or s + 1 <= last(way, a):
                    part[way, a] = partial(a, blk_at(way, a, s + 1))
        weights_of(2 * s - 2)
        weights_of(2 * s - 1)

    def rs_body(s, carry):
        rs_step(s, True)
        return carry

    lax.fori_loop(2, half - 1, rs_body, 0)
    for s in range(max(2, half - 1), half + 1):
        rs_step(s, False)
    out_w = [pltpu.make_async_copy(gw.at[i], ref, ow_sem.at[i]) for i, ref in enumerate((ogg, ogu, ogd))]
    for c in out_w:
        c.start()
    for a in range(2):
        own[a] = partial(a, m)

    sc_all[m] = sc_own[...]
    for c in scores:
        c.wait_recv()
    sc = jnp.sum(sc_all[...], axis=0)[0:1, :]
    sc_col = jnp.sum(jnp.where(p0 == p1, jnp.broadcast_to(sc, (rows, rows)), 0.0), axis=1, keepdims=True)
    hi = sc_col.astype(BF).astype(F32)
    lane = lax.broadcasted_iota(jnp.int32, (rows, 128), 1)
    o_buf[2] = jnp.where(lane == 0, hi, jnp.where(lane == 1, sc_col - hi, 0.0)).astype(BF)

    for a in range(2):
        total = own[a]
        for way in (1 - a, a):
            n = last(way, a)
            turn(way, a, n).wait_recv()
            total = total + rx[way, a, n].astype(F32)
        o_buf[a] = total.astype(BF)

    b1 = send_xc(o_buf, q1, b1_send, b1_recv)
    pending += b1
    for c in b1:
        c.wait_recv()
    for a in range(3):
        q2[a] = dot(swap, q1[a]).astype(BF)
    b2 = send_y(q2, home, b2_send, b2_recv)
    pending += b2

    for c in pending:
        c.wait_send()
    for s in range(1, half + 1):
        for a in range(2):
            for way in range(2):
                if s <= last(way, a):
                    hop(way, a, s).wait_send()
                    turn(way, a, s).wait_send()
    for c in out_w:
        c.wait()
    for c in b2:
        c.wait_recv()

    mixed[...] = (dot(disp_t[0], home[0]) + dot(disp_t[1], home[0])).astype(BF)
    gtok[...] = dot(disp_t[2], home[1]).astype(BF)
    col = home[2].astype(F32)
    col = disp[...] * (col[:, 0:1] + col[:, 1:2])
    for k in range(topk):
        picked = jnp.sum(jnp.where(rt[k : k + 1, :] == e_r, col, 0.0), axis=0, keepdims=True)
        gprob[k : k + 1, :] = picked / pt[k : k + 1, :]


def local(ny, nxc, nz, tokens, routes, probs, w_gate, w_up, w_down, grad_out):
    nt, width = tokens.shape
    topk = routes.shape[1]
    d, f = w_gate.shape[1:]
    rows = ny * nxc * 2
    half = nz // 2
    vmem = pl.BlockSpec(memory_space=pltpu.VMEM)
    hbm = pl.BlockSpec(memory_space=pl.ANY)
    dma = pltpu.SemaphoreType.DMA
    V = pltpu.VMEM
    outs = pl.pallas_call(
        functools.partial(kernel, ny, nxc, nz),
        out_shape=(
            jax.ShapeDtypeStruct((nt, width), BF),
            jax.ShapeDtypeStruct((nt, width), BF),
            jax.ShapeDtypeStruct((topk, nt), F32),
            jax.ShapeDtypeStruct((f, d), BF),
            jax.ShapeDtypeStruct((f, d), BF),
            jax.ShapeDtypeStruct((f, d), BF),
        ),
        in_specs=[vmem] * 4 + [hbm] * 3,
        out_specs=(vmem, vmem, vmem, hbm, hbm, hbm),
        scratch_shapes=[
            V((f, d), BF), V((f, d), BF), V((f, d), BF),
            V((rows, nt), F32), V((3, nt, rows), BF),
            V((2, rows, width), BF), V((2, rows, width), BF), V((2, rows, width), BF),
            V((nz, 2, rows, width), BF),
            V((3, f, rows), F32), V((3, f, rows), BF), V((3, rows, f), BF),
            V((2, 2, rows, width), F32),
            V((2, 2, half + 1, rows, width), BF), V((2, 2, half + 1, rows, width), BF),
            V((2, rows, width), F32),
            V((8, rows), F32), V((nz, 8, rows), F32),
            V((3, rows, width), BF), V((3, rows, width), BF), V((3, rows, width), BF), V((3, rows, width), BF),
            V((3, f, d), BF),
            dma((3,)), dma((3,)),
            dma((ny,)), dma((ny,)), dma((nxc,)), dma((nxc,)),
            dma((2, 2, half + 1)), dma((2, 2, half + 1)), dma((2, 2, half + 1)), dma((2, 2, half + 1)),
            dma((nz,)), dma((nz,)),
            dma((nxc,)), dma((nxc,)), dma((ny,)), dma((ny,)),
        ],
        compiler_params=pltpu.CompilerParams(
            collective_id=0, has_side_effects=True, vmem_limit_bytes=24 * 1024 * 1024
        ),
    )(
        tokens, grad_out, routes.T, probs.T,
        jnp.swapaxes(w_gate, 1, 2).reshape(f, d), jnp.swapaxes(w_up, 1, 2).reshape(f, d), w_down.reshape(f, d),
    )
    mixed, gtok, gprob, gg, gu, gd = outs
    return (
        mixed, gtok, gprob.T,
        jnp.swapaxes(gg.reshape(1, f, d), 1, 2), jnp.swapaxes(gu.reshape(1, f, d), 1, 2), gd.reshape(1, f, d),
    )


def solution(mesh):
    n_exp, nz = mesh.shape["expert"], mesh.shape["mp"]
    ny = 8 if n_exp == 64 else 2
    nxc = n_exp // ny
    placed = (
        P("expert", "mp"),
        P("expert", None),
        P("expert", None),
        P("expert", None, "mp"),
        P("expert", None, "mp"),
        P("expert", "mp", None),
        P("expert", "mp"),
    )
    return jax.shard_map(
        functools.partial(local, ny, nxc, nz),
        mesh=mesh,
        in_specs=placed,
        out_specs=(
            P("expert", "mp"),
            P("expert", "mp"),
            P("expert", None),
            P("expert", None, "mp"),
            P("expert", None, "mp"),
            P("expert", "mp", None),
        ),
        check_vma=False,
    )
```

```python
import functools

import jax
import jax.numpy as jnp
from jax import lax
from jax.experimental import pallas as pl
from jax.experimental.pallas import tpu as pltpu
from jax.sharding import PartitionSpec as P

MESH = pl.DeviceIdType.MESH
BF = jnp.bfloat16
F32 = jnp.float32


def dot(a, b):
    return jnp.dot(a, b, preferred_element_type=F32)


def dot_nt(a, b):
    return lax.dot_general(a, b, (((1,), (1,)), ((), ())), preferred_element_type=F32)


def kernel(
    ny, nxc, nz,
    tok_h, gout_h, rt_h, pt_h, wg_h, wu_h, wd_h,
    mixed, gtok, gprob, gw_g, gw_u, gw_d,
    tok, gout, rt, pt, wg, wu, wd, disp, disp_t, s_buf, r1, b_buf, xg, acc, h_t, h_r, part, tx, rx, own,
    sc_own, sc_all, o_buf, q1, q2, home,
    w_sem, a1_send, a1_recv, a2_send, a2_recv, ag_send, ag_recv, rs_send, rs_recv,
    sc_send, sc_recv, b1_send, b1_recv, b2_send, b2_recv,
):
    e = lax.axis_index("expert")
    m = lax.axis_index("mp")
    x_me = e // (2 * ny)
    y_me = (e // 2) % ny
    xc_me = x_me * 2 + e % 2
    rows = ny * nxc * 2
    nt = tok.shape[0]
    topk = rt.shape[0]

    def y_peer(d):
        y2 = lax.rem(y_me + d, ny)
        return y2, (x_me * ny + y2) * 2 + e % 2

    def xc_peer(d):
        xc2 = lax.rem(xc_me + d, nxc)
        return xc2, ((xc2 // 2) * ny + y_me) * 2 + xc2 % 2

    def z_at(d):
        return lax.rem(m + d + 2 * nz, nz)

    loads = [
        pltpu.make_async_copy(src, dst, w_sem.at[i])
        for i, (src, dst) in enumerate(
            ((rt_h, rt), (pt_h, pt), (tok_h, tok), (gout_h, gout), (wg_h, wg), (wu_h, wu), (wd_h, wd)))
    ]
    for c in loads:
        c.start()

    barrier = pltpu.get_barrier_semaphore()
    for d in range(1, ny):
        pl.semaphore_signal(barrier, inc=1, device_id={"expert": y_peer(d)[1]}, device_id_type=MESH)
    for d in range(1, nxc):
        pl.semaphore_signal(barrier, inc=1, device_id={"expert": xc_peer(d)[1]}, device_id_type=MESH)
    for d in range(1, nz):
        pl.semaphore_signal(barrier, inc=1, device_id={"mp": z_at(d)}, device_id_type=MESH)

    for c in loads[:4]:
        c.wait()
    r = lax.broadcasted_iota(jnp.int32, (rows, nt), 0)
    sy = nxc * 2
    y_r = r // sy
    xc_r = (r % sy) // 2
    slot_r = r % 2
    e_r = (xc_r // 2) * (2 * ny) + y_r * 2 + xc_r % 2
    chosen = jnp.zeros((rows, nt), F32)
    weight = jnp.zeros((rows, nt), F32)
    for k in range(topk):
        hit = rt[k : k + 1, :] == e_r
        chosen = jnp.where(hit, 1.0, chosen)
        weight = jnp.where(hit, pt[k : k + 1, :], weight)
    t0 = lax.broadcasted_iota(jnp.int32, (nt, nt), 0)
    t1 = lax.broadcasted_iota(jnp.int32, (nt, nt), 1)
    earlier = jnp.where(t0 < t1, 1.0, 0.0).astype(BF)
    before = dot(chosen.astype(BF), earlier)
    d_f = jnp.where(before == slot_r.astype(F32), chosen, 0.0)
    d_w = d_f * weight
    disp[...] = d_f
    d_b = d_f.astype(BF)
    w_row = jnp.sum(d_w, axis=1, keepdims=True)
    s_buf[0] = dot(d_b, tok[...]).astype(BF)
    s_buf[1] = (dot(d_b, gout[...]) * w_row).astype(BF)

    pl.semaphore_wait(barrier, (ny - 1) + (nxc - 1) + (nz - 1))

    def chunk(i, n):
        return pl.ds(pl.multiple_of(i * n, n), n)

    def send_y(src, dst, ss, rs):
        copies = []
        for d in range(1, ny):
            y2, peer = y_peer(d)
            c = pltpu.make_async_remote_copy(
                src_ref=src.at[:, chunk(y2, sy), :], dst_ref=dst.at[:, chunk(y_me, sy), :],
                send_sem=ss.at[d], recv_sem=rs.at[d], device_id={"expert": peer}, device_id_type=MESH)
            c.start()
            copies.append(c)
        dst[:, chunk(y_me, sy), :] = src[:, chunk(y_me, sy), :]
        return copies

    sx = ny * 2

    def send_xc(src, dst, ss, rs):
        copies = []
        for d in range(1, nxc):
            xc2, peer = xc_peer(d)
            c = pltpu.make_async_remote_copy(
                src_ref=src.at[:, chunk(xc2, sx), :], dst_ref=dst.at[:, chunk(xc_me, sx), :],
                send_sem=ss.at[d], recv_sem=rs.at[d], device_id={"expert": peer}, device_id_type=MESH)
            c.start()
            copies.append(c)
        dst[:, chunk(xc_me, sx), :] = src[:, chunk(xc_me, sx), :]
        return copies

    pending = []

    a1 = send_y(s_buf, r1, a1_send, a1_recv)
    pending += a1

    t_f = jnp.transpose(d_f)
    t_w = jnp.transpose(d_w)
    t_hi = t_w.astype(BF)
    disp_t[0] = t_hi
    disp_t[1] = (t_w - t_hi.astype(F32)).astype(BF)
    disp_t[2] = t_f.astype(BF)
    p0 = lax.broadcasted_iota(jnp.int32, (rows, rows), 0)
    p1 = lax.broadcasted_iota(jnp.int32, (rows, rows), 1)
    source = ((p0 % sx) // 2) * sy + (p0 // sx) * 2 + p0 % 2
    swap = jnp.where(p1 == source, 1.0, 0.0).astype(BF)
    for a in range(3):
        acc[a] = jnp.zeros(acc.shape[1:], F32)

    for c in a1:
        c.wait_recv()
    for a in range(2):
        b_buf[a] = dot(swap, r1[a]).astype(BF)

    a2 = send_xc(b_buf, xg.at[m], a2_send, a2_recv)
    pending += a2
    for c in loads[4:]:
        c.wait()
    for c in a2:
        c.wait_recv()

    def give(a, o, to):
        blk = z_at(-o)
        return pltpu.make_async_remote_copy(
            src_ref=xg.at[blk, a], dst_ref=xg.at[blk, a],
            send_sem=ag_send.at[a, to % nz], recv_sem=ag_recv.at[a, to % nz],
            device_id={"mp": z_at(to - o)}, device_id_type=MESH)

    def got(a, o):
        blk = z_at(-o)
        pltpu.make_async_remote_copy(
            src_ref=xg.at[blk, a], dst_ref=xg.at[blk, a],
            send_sem=ag_send.at[a, o % nz], recv_sem=ag_recv.at[a, o % nz],
            device_id={"mp": z_at(1)}, device_id_type=MESH).wait_recv()

    def cols(blk):
        return pl.ds(pl.multiple_of(blk * 128, 128), 128)

    def use(blk, a):
        v = xg[blk, a]
        if a == 0:
            acc[0] += dot_nt(wg[:, cols(blk)], v)
            acc[1] += dot_nt(wu[:, cols(blk)], v)
        else:
            acc[2] += dot_nt(wd[:, cols(blk)], v)

    def far(a):
        return 8 if a == 0 else -8

    for to in (3, -3, 1, -1):
        for a in range(2):
            give(a, 0, to).start()

    def use_at(o):
        for a in range(2):
            use(z_at(-o), a)

    use_at(0)
    for a in range(2):
        for g in (1, -1):
            got(a, 3 * g)
            for to in (6, 4, 2):
                give(a, 3 * g, to * g).start()
    for o in (3, -3):
        use_at(o)
    for o in (1, -1):
        for a in range(2):
            got(a, o)
        use_at(o)
    for a in range(2):
        for g in (1, -1):
            got(a, 6 * g)
            if far(a) * g > 0:
                give(a, 6 * g, 8 * g).start()
            for to in (7, 5):
                give(a, 6 * g, to * g).start()

    def use_many(base, n):
        def body(i, carry):
            o = (1 - 2 * (i % 2)) * (base + 2 * (i // 2))
            for a in range(2):
                got(a, o)
            for a in range(2):
                use(z_at(-o), a)
            return carry

        lax.fori_loop(0, n, body, 0)

    use_many(2, 4)
    for o in (6, -6):
        use_at(o)
    use_many(5, 4)
    for a in range(2):
        got(a, far(a))
        use(z_at(-far(a)), a)

    gate, up, back = acc[0], acc[1], acc[2]
    sig = jax.nn.sigmoid(gate)
    silu = gate * sig
    hid = silu * up
    u_g = back * silu
    g_g = back * up * sig * (1.0 + gate * (1.0 - sig))
    sc_own[...] = jnp.broadcast_to(jnp.sum(hid * back, axis=0, keepdims=True), sc_own.shape)
    scores = []
    for d in range(1, nz):
        c = pltpu.make_async_remote_copy(
            src_ref=sc_own, dst_ref=sc_all.at[m], send_sem=sc_send.at[d], recv_sem=sc_recv.at[d],
            device_id={"mp": z_at(d)}, device_id_type=MESH)
        c.start()
        scores.append(c)
    pending += scores
    for i, v in enumerate((hid, g_g, u_g)):
        h_r[i] = jnp.transpose(v).astype(BF)
        h_t[i] = v.astype(BF)

    def partial(a, blk):
        if a == 0:
            return dot(h_r[0], wd[:, cols(blk)])
        return dot(h_r[1], wg[:, cols(blk)]) + dot(h_r[2], wu[:, cols(blk)])

    def turn(a, o, to):
        return pltpu.make_async_remote_copy(
            src_ref=tx.at[a, o % nz], dst_ref=rx.at[a, o % nz],
            send_sem=rs_send.at[a, o % nz], recv_sem=rs_recv.at[a, o % nz],
            device_id={"mp": z_at(to - o)}, device_id_type=MESH)

    def came(a, o):
        turn(a, o, o + 1).wait_recv()
        return rx[a, o % nz].astype(F32)

    def weights_of(blk):
        x_v, g_v = xg[blk, 0], xg[blk, 1]
        gw_g[:, cols(blk)] = dot(h_t[1], x_v).astype(BF)
        gw_u[:, cols(blk)] = dot(h_t[2], x_v).astype(BF)
        gw_d[:, cols(blk)] = dot(h_t[0], g_v).astype(BF)

    def weights_from(first, last):
        def body(i, carry):
            weights_of(i)
            return carry

        lax.fori_loop(first, last, body, 0)

    def leaf(a, o, to):
        tx[a, o % nz] = partial(a, z_at(-o)).astype(BF)
        turn(a, o, to).start()

    def leaves(centre):
        def body(i, carry):
            g = 1 - 2 * (i % 2)
            o = g * (centre - 1 + 2 * (i // 2))
            for a in range(2):
                leaf(a, o, g * centre)
            return carry

        lax.fori_loop(0, 4, body, 0)

    for a in range(2):
        leaf(a, far(a), far(a) * 6 // 8)
    leaves(6)
    leaves(3)
    for g in range(2):
        for a in range(2):
            part[g, a] = partial(a, z_at((-6, 6)[g]))
    for a in range(2):
        for g in range(2):
            sign = (1, -1)[g]
            total = part[g, a] + came(a, 5 * sign) + came(a, 7 * sign)
            if far(a) * sign > 0:
                total = total + came(a, 8 * sign)
            tx[a, 6 * sign % nz] = total.astype(BF)
            turn(a, 6 * sign, 3 * sign).start()
    for g in range(2):
        for a in range(2):
            leaf(a, (1, -1)[g], 0)
            part[g, a] = partial(a, z_at((-3, 3)[g]))
    weights_from(0, 6)
    for a in range(2):
        for g in range(2):
            sign = (1, -1)[g]
            total = part[g, a] + came(a, 2 * sign) + came(a, 4 * sign) + came(a, 6 * sign)
            tx[a, 3 * sign % nz] = total.astype(BF)
            turn(a, 3 * sign, 0).start()
    for a in range(2):
        own[a] = partial(a, m)
    weights_from(6, 16)

    sc_all[m] = sc_own[...]
    for c in scores:
        c.wait_recv()
    sc = jnp.sum(sc_all[...], axis=0)[0:1, :]
    sc_col = jnp.sum(jnp.where(p0 == p1, jnp.broadcast_to(sc, (rows, rows)), 0.0), axis=1, keepdims=True)
    hi = sc_col.astype(BF).astype(F32)
    lane = lax.broadcasted_iota(jnp.int32, (rows, 128), 1)
    o_buf[2] = jnp.where(lane == 0, hi, jnp.where(lane == 1, sc_col - hi, 0.0)).astype(BF)

    for a in range(2):
        total = own[a]
        for o in (1, -1, 3, -3):
            total = total + came(a, o)
        o_buf[a] = total.astype(BF)

    b1 = send_xc(o_buf, q1, b1_send, b1_recv)
    pending += b1
    for c in b1:
        c.wait_recv()
    for a in range(3):
        q2[a] = dot(swap, q1[a]).astype(BF)
    b2 = send_y(q2, home, b2_send, b2_recv)
    pending += b2

    for c in pending:
        c.wait_send()
    for o in range(1, nz):
        for a in range(2):
            give(a, 0, o).wait_send()
            turn(a, o, 0).wait_send()
    for c in b2:
        c.wait_recv()

    mixed[...] = (dot(disp_t[0], home[0]) + dot(disp_t[1], home[0])).astype(BF)
    gtok[...] = dot(disp_t[2], home[1]).astype(BF)
    col = home[2].astype(F32)
    col = disp[...] * (col[:, 0:1] + col[:, 1:2])
    for k in range(topk):
        picked = jnp.sum(jnp.where(rt[k : k + 1, :] == e_r, col, 0.0), axis=0, keepdims=True)
        gprob[k : k + 1, :] = picked / pt[k : k + 1, :]


def write_out(*refs):
    n = len(refs) // 2
    sems = refs[-1]
    copies = [pltpu.make_async_copy(refs[i], refs[n + i], sems.at[i]) for i in range(n)]
    for c in copies:
        c.start()
    for c in copies:
        c.wait()


def local(ny, nxc, nz, tokens, routes, probs, w_gate, w_up, w_down, grad_out):
    nt, width = tokens.shape
    topk = routes.shape[1]
    d, f = w_gate.shape[1:]
    rows = ny * nxc * 2
    vmem = pl.BlockSpec(memory_space=pltpu.VMEM)
    hbm = pl.BlockSpec(memory_space=pl.ANY)
    dma = pltpu.SemaphoreType.DMA
    V = pltpu.VMEM
    shapes = (
        jax.ShapeDtypeStruct((nt, width), BF),
        jax.ShapeDtypeStruct((nt, width), BF),
        jax.ShapeDtypeStruct((topk, nt), F32),
        jax.ShapeDtypeStruct((f, d), BF),
        jax.ShapeDtypeStruct((f, d), BF),
        jax.ShapeDtypeStruct((f, d), BF),
    )
    outs = pl.pallas_call(
        functools.partial(kernel, ny, nxc, nz),
        out_shape=tuple(pltpu.VMEM(t.shape, t.dtype) for t in shapes),
        in_specs=[hbm] * 7,
        out_specs=(vmem,) * 6,
        scratch_shapes=[
            V((nt, width), BF), V((nt, width), BF), V((topk, nt), jnp.int32), V((topk, nt), F32),
            V((f, d), BF), V((f, d), BF), V((f, d), BF),
            V((rows, nt), F32), V((3, nt, rows), BF),
            V((2, rows, width), BF), V((2, rows, width), BF), V((2, rows, width), BF),
            V((nz, 2, rows, width), BF),
            V((3, f, rows), F32), V((3, f, rows), BF), V((3, rows, f), BF),
            V((2, 2, rows, width), F32),
            V((2, nz, rows, width), BF), V((2, nz, rows, width), BF),
            V((2, rows, width), F32),
            V((8, rows), F32), V((nz, 8, rows), F32),
            V((3, rows, width), BF), V((3, rows, width), BF), V((3, rows, width), BF), V((3, rows, width), BF),
            dma((7,)),
            dma((ny,)), dma((ny,)), dma((nxc,)), dma((nxc,)),
            dma((2, nz)), dma((2, nz)), dma((2, nz)), dma((2, nz)),
            dma((nz,)), dma((nz,)),
            dma((nxc,)), dma((nxc,)), dma((ny,)), dma((ny,)),
        ],
        compiler_params=pltpu.CompilerParams(
            collective_id=0, has_side_effects=True, vmem_limit_bytes=65700000
        ),
    )(
        tokens, grad_out, routes.T, probs.T,
        jnp.swapaxes(w_gate, 1, 2).reshape(f, d), jnp.swapaxes(w_up, 1, 2).reshape(f, d), w_down.reshape(f, d),
    )
    outs = pl.pallas_call(
        write_out,
        out_shape=shapes,
        in_specs=[hbm] * 6,
        out_specs=(pl.BlockSpec(memory_space=pltpu.HBM),) * 6,
        scratch_shapes=[dma((6,))],
        compiler_params=pltpu.CompilerParams(vmem_limit_bytes=1024 * 1024),
    )(*outs)
    mixed, gtok, gprob, gg, gu, gd = outs
    return (
        mixed, gtok, gprob.T,
        jnp.swapaxes(gg.reshape(1, f, d), 1, 2), jnp.swapaxes(gu.reshape(1, f, d), 1, 2), gd.reshape(1, f, d),
    )


def solution(mesh):
    n_exp, nz = mesh.shape["expert"], mesh.shape["mp"]
    ny = 8 if n_exp == 64 else 2
    nxc = n_exp // ny
    placed = (
        P("expert", "mp"),
        P("expert", None),
        P("expert", None),
        P("expert", None, "mp"),
        P("expert", None, "mp"),
        P("expert", "mp", None),
        P("expert", "mp"),
    )
    return jax.shard_map(
        functools.partial(local, ny, nxc, nz),
        mesh=mesh,
        in_specs=placed,
        out_specs=(
            P("expert", "mp"),
            P("expert", "mp"),
            P("expert", None),
            P("expert", None, "mp"),
            P("expert", None, "mp"),
            P("expert", "mp", None),
        ),
        check_vma=False,
    )
```

```python
import functools

import jax
import jax.numpy as jnp
from jax import lax
from jax.experimental import pallas as pl
from jax.experimental.pallas import tpu as pltpu
from jax.sharding import PartitionSpec as P

MESH = pl.DeviceIdType.MESH
BF = jnp.bfloat16
F32 = jnp.float32


def dot(a, b):
    return jnp.dot(a, b, preferred_element_type=F32)


def dot_nt(a, b):
    return lax.dot_general(a, b, (((1,), (1,)), ((), ())), preferred_element_type=F32)


def kernel(
    ne, nz,
    tok_h, gout_h, rt_h, pt_h, wg_h, wu_h, wd_h,
    mixed, gtok, gprob, gw_g, gw_u, gw_d,
    tok, gout, rt, pt, wg, wu, wd, disp, disp_t, s_buf, r_buf, xg, acc, h_t, h_r, part, tx, rx, own,
    sc_all, o_buf, o_home, b_buf, b_home,
    w_sem, a2a_send, a2a_recv, ag_send, ag_recv, rs_send, rs_recv, sc_send, sc_recv,
):
    e = lax.axis_index("expert")
    m = lax.axis_index("mp")
    rows = 2 * ne
    nt = tok.shape[0]
    topk = rt.shape[0]

    def z_at(d):
        return lax.rem(m + d + 2 * nz, nz)

    loads = [
        pltpu.make_async_copy(src, dst, w_sem.at[i])
        for i, (src, dst) in enumerate(
            ((rt_h, rt), (pt_h, pt), (tok_h, tok), (gout_h, gout), (wg_h, wg), (wu_h, wu), (wd_h, wd)))
    ]
    for c in loads:
        c.start()

    barrier = pltpu.get_barrier_semaphore()
    def greet(d, carry):
        pl.semaphore_signal(barrier, inc=1, device_id={"expert": lax.rem(e + d, ne)}, device_id_type=MESH)
        return carry

    lax.fori_loop(1, ne, greet, 0)
    near = (1, -1, 2, -2, 3, -3)
    for d in near:
        pl.semaphore_signal(barrier, inc=1, device_id={"mp": z_at(d)}, device_id_type=MESH)

    for c in loads[:4]:
        c.wait()
    r = lax.broadcasted_iota(jnp.int32, (rows, nt), 0)
    slot_r = r // ne
    e_r = r % ne
    chosen = jnp.zeros((rows, nt), F32)
    weight = jnp.zeros((rows, nt), F32)
    for k in range(topk):
        hit = rt[k : k + 1, :] == e_r
        chosen = jnp.where(hit, 1.0, chosen)
        weight = jnp.where(hit, pt[k : k + 1, :], weight)
    t0 = lax.broadcasted_iota(jnp.int32, (nt, nt), 0)
    t1 = lax.broadcasted_iota(jnp.int32, (nt, nt), 1)
    earlier = jnp.where(t0 < t1, 1.0, 0.0).astype(BF)
    before = dot(chosen.astype(BF), earlier)
    d_f = jnp.where(before == slot_r.astype(F32), chosen, 0.0)
    d_w = d_f * weight
    disp[...] = d_f
    d_b = d_f.astype(BF)
    w_row = jnp.sum(d_w, axis=1, keepdims=True)
    v_in = dot(d_b, tok[...])
    v_grad = dot(d_b, gout[...]) * w_row

    def put(ref, i, v):
        ref[:, 0, 128 * i : 128 * (i + 1)] = v[:ne]
        ref[:, 0, 128 * (i + 1) : 128 * (i + 2)] = v[ne:]

    def take(ref, i):
        return jnp.concatenate(
            [ref[:, 0, 128 * i : 128 * (i + 1)], ref[:, 0, 128 * (i + 1) : 128 * (i + 2)]], axis=0).astype(BF)

    put(s_buf, 0, v_in)
    put(s_buf, 2, v_grad)

    pl.semaphore_wait(barrier, (ne - 1) + len(near))

    def to_all(i, src, dst):
        def body(d, carry):
            peer = lax.rem(e + d, ne)
            pltpu.make_async_remote_copy(
                src_ref=src.at[peer], dst_ref=dst.at[e], send_sem=a2a_send.at[i], recv_sem=a2a_recv.at[i],
                device_id={"expert": peer}, device_id_type=MESH).start()
            return carry

        lax.fori_loop(1, ne, body, 0)
        dst[e] = src[e]

    def all_of(i, src, dst):
        return pltpu.make_async_remote_copy(
            src_ref=src.at[pl.ds(0, ne - 1)], dst_ref=dst.at[pl.ds(0, ne - 1)],
            send_sem=a2a_send.at[i], recv_sem=a2a_recv.at[i],
            device_id={"expert": lax.rem(e + 1, ne)}, device_id_type=MESH)

    to_all(0, s_buf, r_buf)

    t_f = jnp.transpose(d_f)
    t_w = jnp.transpose(d_w)
    t_hi = t_w.astype(BF)
    disp_t[0] = t_hi
    disp_t[1] = (t_w - t_hi.astype(F32)).astype(BF)
    disp_t[2] = t_f.astype(BF)
    for a in range(3):
        acc[a] = jnp.zeros(acc.shape[1:], F32)

    for c in loads[4:]:
        c.wait()
    all_of(0, s_buf, r_buf).wait_recv()
    for a in range(2):
        xg[m, a] = take(r_buf, 2 * a)

    def give(a, o, to):
        blk = z_at(-o)
        return pltpu.make_async_remote_copy(
            src_ref=xg.at[blk, a], dst_ref=xg.at[blk, a],
            send_sem=ag_send.at[a, to % nz], recv_sem=ag_recv.at[a, to % nz],
            device_id={"mp": z_at(to - o)}, device_id_type=MESH)

    def got(a, o):
        blk = z_at(-o)
        pltpu.make_async_remote_copy(
            src_ref=xg.at[blk, a], dst_ref=xg.at[blk, a],
            send_sem=ag_send.at[a, o % nz], recv_sem=ag_recv.at[a, o % nz],
            device_id={"mp": z_at(1)}, device_id_type=MESH).wait_recv()

    def cols(blk):
        return pl.ds(pl.multiple_of(blk * 128, 128), 128)

    def use(blk, a):
        v = xg[blk, a]
        if a == 0:
            acc[0] += dot_nt(wg[:, cols(blk)], v)
            acc[1] += dot_nt(wu[:, cols(blk)], v)
        else:
            acc[2] += dot_nt(wd[:, cols(blk)], v)

    def far(a):
        return 8 if a == 0 else -8

    def pass3(a):
        for g in (1, -1):
            got(a, 3 * g)
            for to in (6, 4, 2):
                give(a, 3 * g, to * g).start()

    def pass6(a):
        for g in (1, -1):
            got(a, 6 * g)
            if far(a) * g > 0:
                give(a, 6 * g, 8 * g).start()
            for to in (7, 5):
                give(a, 6 * g, to * g).start()

    def use_at(a, *offsets):
        for o in offsets:
            use(z_at(-o), a)

    def use_many(a, base, n):
        def body(i, carry):
            o = (1 - 2 * (i % 2)) * (base + 2 * (i // 2))
            got(a, o)
            use(z_at(-o), a)
            return carry

        lax.fori_loop(0, n, body, 0)

    for a in range(2):
        for to in (3, -3, 1, -1):
            give(a, 0, to).start()
    use_at(0, 0)
    pass3(0)
    use_at(0, 3, -3)
    pass3(1)
    use_many(0, 1, 2)
    use_at(1, 0, 3, -3)
    pass6(0)
    use_many(0, 2, 4)
    use_at(0, 6, -6)
    pass6(1)
    use_many(0, 5, 4)
    got(0, far(0))
    use_at(0, far(0))

    def keep(i, v):
        h_r[i] = jnp.transpose(v).astype(BF)
        h_t[i] = v.astype(BF)

    gate, up = acc[0], acc[1]
    keep(0, gate * jax.nn.sigmoid(gate) * up)

    def partial(a, blk):
        if a == 0:
            return dot(h_r[0], wd[:, cols(blk)])
        return dot(h_r[1], wg[:, cols(blk)]) + dot(h_r[2], wu[:, cols(blk)])

    def turn(a, o, to):
        return pltpu.make_async_remote_copy(
            src_ref=tx.at[a, o % nz], dst_ref=rx.at[a, o % nz],
            send_sem=rs_send.at[a, o % nz], recv_sem=rs_recv.at[a, o % nz],
            device_id={"mp": z_at(to - o)}, device_id_type=MESH)

    def came(a, o):
        turn(a, o, o + 1).wait_recv()
        return rx[a, o % nz].astype(F32)

    def weights_of(blk):
        x_v, g_v = xg[blk, 0], xg[blk, 1]
        gw_g[:, cols(blk)] = dot(h_t[1], x_v).astype(BF)
        gw_u[:, cols(blk)] = dot(h_t[2], x_v).astype(BF)
        gw_d[:, cols(blk)] = dot(h_t[0], g_v).astype(BF)

    def weights_from(first, last):
        def body(i, carry):
            weights_of(i)
            return carry

        lax.fori_loop(first, last, body, 0)

    def leaf(a, o, to):
        tx[a, o % nz] = partial(a, z_at(-o)).astype(BF)
        turn(a, o, to).start()

    def leaves(a):
        leaf(a, far(a), far(a) * 6 // 8)

        def body(i, carry):
            g = 1 - 2 * (i % 2)
            centre = 6 - 3 * (i // 4)
            o = centre - 1 + 2 * ((i // 2) % 2)
            leaf(a, g * o, g * centre)
            return carry

        lax.fori_loop(0, 8, body, 0)

    def leaves1(a):
        for g in (1, -1):
            leaf(a, g, 0)

    def part_of(a, o):
        for g in range(2):
            part[g, a] = partial(a, z_at((-o, o)[g]))

    def mid(a, o, to, kids):
        for g in range(2):
            sign = (1, -1)[g]
            total = part[g, a]
            for k in kids:
                if k < 8 or far(a) * sign > 0:
                    total = total + came(a, k * sign)
            tx[a, o * sign % nz] = total.astype(BF)
            turn(a, o * sign, to * sign).start()

    def final(a):
        total = own[a]
        for o in (1, -1, 3, -3):
            total = total + came(a, o)
        put((o_buf, b_buf)[a], 0, total)

    def give_sc(o, to):
        return pltpu.make_async_remote_copy(
            src_ref=sc_all.at[z_at(-o)], dst_ref=sc_all.at[z_at(-o)],
            send_sem=sc_send.at[to % nz], recv_sem=sc_recv.at[to % nz],
            device_id={"mp": z_at(to - o)}, device_id_type=MESH)

    def got_sc(o):
        pltpu.make_async_remote_copy(
            src_ref=sc_all.at[z_at(-o)], dst_ref=sc_all.at[z_at(-o)],
            send_sem=sc_send.at[o % nz], recv_sem=sc_recv.at[o % nz],
            device_id={"mp": z_at(1)}, device_id_type=MESH).wait_recv()

    leaves(0)
    leaves1(0)
    part_of(0, 6)

    use_many(1, 1, 2)
    use_many(1, 2, 4)
    use_at(1, 6, -6)
    use_many(1, 5, 4)
    got(1, far(1))
    use_at(1, far(1))
    gate, up, back = acc[0], acc[1], acc[2]
    sig = jax.nn.sigmoid(gate)
    silu = gate * sig
    keep(1, back * up * sig * (1.0 + gate * (1.0 - sig)))
    keep(2, back * silu)
    mid(0, 6, 3, (5, 7, 8))
    sc_all[m] = jnp.broadcast_to(jnp.sum(silu * up * back, axis=0, keepdims=True), sc_all.shape[1:])
    leaves(1)
    for to in (3, -3, 1, -1):
        give_sc(0, to).start()
    part_of(0, 3)
    part_of(1, 6)
    mid(0, 3, 0, (2, 4, 6))
    mid(1, 6, 3, (5, 7, 8))
    leaves1(1)
    for g in (1, -1):
        got_sc(3 * g)
        for to in (6, 4, 2):
            give_sc(3 * g, to * g).start()
    part_of(1, 3)
    for a in range(2):
        own[a] = partial(a, m)
    weights_from(0, 5)

    final(0)
    to_all(1, o_buf, o_home)
    mid(1, 3, 0, (2, 4, 6))
    for g in (1, -1):
        got_sc(6 * g)
        for to in (7, 5):
            give_sc(6 * g, to * g).start()
    give_sc(6, 8).start()
    weights_from(5, 16)

    for o in (1, -1, 2, -2, 4, -4, 5, -5, 7, -7, 8):
        got_sc(o)
    sc = jnp.broadcast_to(jnp.sum(sc_all[...], axis=0)[0:1, :], (ne, rows))
    row = lax.broadcasted_iota(jnp.int32, (ne, rows), 0)
    col = lax.broadcasted_iota(jnp.int32, (ne, rows), 1)
    sc_col = [jnp.sum(jnp.where(col == row + ne * i, sc, 0.0), axis=1, keepdims=True) for i in range(2)]
    lane = lax.broadcasted_iota(jnp.int32, (ne, 128), 1)
    b_buf[:, 0, 256:384] = jnp.where(lane == 0, sc_col[0], jnp.where(lane == 1, sc_col[1], 0.0))

    final(1)
    to_all(2, b_buf, b_home)

    all_of(1, o_buf, o_home).wait_recv()
    out = take(o_home, 0)
    mixed[...] = (dot(disp_t[0], out) + dot(disp_t[1], out)).astype(BF)

    for i, refs in enumerate(((s_buf, r_buf), (o_buf, o_home), (b_buf, b_home))):
        all_of(i, *refs).wait_send()
    for o in range(1, nz):
        for a in range(2):
            give(a, 0, o).wait_send()
            turn(a, o, 0).wait_send()
        give_sc(0, o).wait_send()
    all_of(2, b_buf, b_home).wait_recv()

    gtok[...] = dot(disp_t[2], take(b_home, 0)).astype(BF)
    score = b_home[:, 0, 256:384]
    score = disp[...] * jnp.concatenate([score[:, 0:1], score[:, 1:2]], axis=0)
    for k in range(topk):
        picked = jnp.sum(jnp.where(rt[k : k + 1, :] == e_r, score, 0.0), axis=0, keepdims=True)
        gprob[k : k + 1, :] = picked / pt[k : k + 1, :]


def write_out(*refs):
    n = len(refs) // 2
    sems = refs[-1]
    copies = [pltpu.make_async_copy(refs[i], refs[n + i], sems.at[i]) for i in range(n)]
    for c in copies:
        c.start()
    for c in copies:
        c.wait()


def local(ne, nz, tokens, routes, probs, w_gate, w_up, w_down, grad_out):
    nt, width = tokens.shape
    topk = routes.shape[1]
    d, f = w_gate.shape[1:]
    rows = ne * 2
    vmem = pl.BlockSpec(memory_space=pltpu.VMEM)
    hbm = pl.BlockSpec(memory_space=pl.ANY)
    dma = pltpu.SemaphoreType.DMA
    V = pltpu.VMEM
    shapes = (
        jax.ShapeDtypeStruct((nt, width), BF),
        jax.ShapeDtypeStruct((nt, width), BF),
        jax.ShapeDtypeStruct((topk, nt), F32),
        jax.ShapeDtypeStruct((f, d), BF),
        jax.ShapeDtypeStruct((f, d), BF),
        jax.ShapeDtypeStruct((f, d), BF),
    )
    outs = pl.pallas_call(
        functools.partial(kernel, ne, nz),
        out_shape=tuple(pltpu.VMEM(t.shape, t.dtype) for t in shapes),
        in_specs=[hbm] * 7,
        out_specs=(vmem,) * 6,
        scratch_shapes=[
            V((nt, width), BF), V((nt, width), BF), V((topk, nt), jnp.int32), V((topk, nt), F32),
            V((f, d), BF), V((f, d), BF), V((f, d), BF),
            V((rows, nt), F32), V((3, nt, rows), BF),
            V((ne, 1, 512), F32), V((ne, 1, 512), F32),
            V((nz, 2, rows, width), BF),
            V((3, f, rows), F32), V((3, f, rows), BF), V((3, rows, f), BF),
            V((2, 2, rows, width), F32),
            V((2, nz, rows, width), BF), V((2, nz, rows, width), BF),
            V((2, rows, width), F32),
            V((nz, 8, rows), F32),
            V((ne, 1, 256), F32), V((ne, 1, 256), F32), V((ne, 1, 384), F32), V((ne, 1, 384), F32),
            dma((7,)), dma((3,)), dma((3,)),
            dma((2, nz)), dma((2, nz)), dma((2, nz)), dma((2, nz)),
            dma((nz,)), dma((nz,)),
        ],
        compiler_params=pltpu.CompilerParams(
            collective_id=0, has_side_effects=True, vmem_limit_bytes=65700000
        ),
    )(
        tokens, grad_out, routes.T, probs.T,
        jnp.swapaxes(w_gate, 1, 2).reshape(f, d), jnp.swapaxes(w_up, 1, 2).reshape(f, d), w_down.reshape(f, d),
    )
    outs = pl.pallas_call(
        write_out,
        out_shape=shapes,
        in_specs=[hbm] * 6,
        out_specs=(pl.BlockSpec(memory_space=pltpu.HBM),) * 6,
        scratch_shapes=[dma((6,))],
        compiler_params=pltpu.CompilerParams(vmem_limit_bytes=1024 * 1024),
    )(*outs)
    mixed, gtok, gprob, gg, gu, gd = outs
    return (
        mixed, gtok, gprob.T,
        jnp.swapaxes(gg.reshape(1, f, d), 1, 2), jnp.swapaxes(gu.reshape(1, f, d), 1, 2), gd.reshape(1, f, d),
    )


def solution(mesh):
    ne, nz = mesh.shape["expert"], mesh.shape["mp"]
    placed = (
        P("expert", "mp"),
        P("expert", None),
        P("expert", None),
        P("expert", None, "mp"),
        P("expert", None, "mp"),
        P("expert", "mp", None),
        P("expert", "mp"),
    )
    return jax.shard_map(
        functools.partial(local, ne, nz),
        mesh=mesh,
        in_specs=placed,
        out_specs=(
            P("expert", "mp"),
            P("expert", "mp"),
            P("expert", None),
            P("expert", None, "mp"),
            P("expert", None, "mp"),
            P("expert", "mp", None),
        ),
        check_vma=False,
    )
```

```python
import functools

import jax
import jax.numpy as jnp
from jax import lax
from jax.experimental import pallas as pl
from jax.experimental.pallas import tpu as pltpu
from jax.sharding import PartitionSpec as P

MESH = pl.DeviceIdType.MESH
BF = jnp.bfloat16
F32 = jnp.float32


def dot(a, b):
    return jnp.dot(a, b, preferred_element_type=F32)


def dot_nt(a, b):
    return lax.dot_general(a, b, (((1,), (1,)), ((), ())), preferred_element_type=F32)


def kernel(
    ne, nz,
    tok_h, gout_h, rt_h, pt_h, wg_h, wu_h, wd_h,
    mixed, gtok, gprob, gw_g, gw_u, gw_d,
    tok, gout, rt, pt, wg, wu, wd, disp, disp_t, s_in, s_grad, r_in, r_grad, xg, acc, h_t, h_r, part, tx, rx, own,
    sc_all, o_buf, o_home, b_buf, b_home,
    w_sem, a2a_send, a2a_recv, ag_send, ag_recv, rs_send, rs_recv, sc_send, sc_recv,
):
    e = lax.axis_index("expert")
    m = lax.axis_index("mp")
    rows = 2 * ne
    nt = tok.shape[0]
    topk = rt.shape[0]

    def z_at(d):
        return lax.rem(m + d + 2 * nz, nz)

    loads = [
        pltpu.make_async_copy(src, dst, w_sem.at[i])
        for i, (src, dst) in enumerate(
            ((rt_h, rt), (pt_h, pt), (tok_h, tok), (gout_h, gout), (wg_h, wg), (wu_h, wu), (wd_h, wd)))
    ]
    for c in loads:
        c.start()

    barrier = pltpu.get_barrier_semaphore()
    def each_peer(act):
        far_half = ne // 2
        n = 4 if far_half % 4 == 0 else 1

        def ahead(i, carry):
            for j in range(n):
                act(lax.rem(e + far_half + n * i + j, ne))
            return carry

        def behind(i, carry):
            for j in range(n):
                act(lax.rem(e + far_half - 1 - n * i - j, ne))
            return carry

        lax.fori_loop(0, far_half // n, ahead, 0)
        lax.fori_loop(0, far_half // n - 1, behind, 0)
        for d in range(n - 1, 0, -1):
            act(lax.rem(e + d, ne))

    each_peer(lambda peer: pl.semaphore_signal(
        barrier, inc=1, device_id={"expert": peer}, device_id_type=MESH))
    near = (1, -1, 2, -2, 3, -3)
    for d in near:
        pl.semaphore_signal(barrier, inc=1, device_id={"mp": z_at(d)}, device_id_type=MESH)

    for c in loads[:4]:
        c.wait()
    r = lax.broadcasted_iota(jnp.int32, (rows, nt), 0)
    slot_r = r // ne
    e_r = r % ne
    chosen = jnp.zeros((rows, nt), F32)
    weight = jnp.zeros((rows, nt), F32)
    for k in range(topk):
        hit = rt[k : k + 1, :] == e_r
        chosen = jnp.where(hit, 1.0, chosen)
        weight = jnp.where(hit, pt[k : k + 1, :], weight)
    t0 = lax.broadcasted_iota(jnp.int32, (nt, nt), 0)
    t1 = lax.broadcasted_iota(jnp.int32, (nt, nt), 1)
    earlier = jnp.where(t0 < t1, 1.0, 0.0).astype(BF)
    before = dot(chosen.astype(BF), earlier)
    d_f = jnp.where(before == slot_r.astype(F32), chosen, 0.0)
    d_w = d_f * weight
    disp[...] = d_f
    d_b = d_f.astype(BF)
    w_row = jnp.sum(d_w, axis=1, keepdims=True)
    v_in = dot(d_b, tok[...])
    v_grad = dot(d_b, gout[...]) * w_row

    def put(ref, i, v):
        ref[:, 0, 128 * i : 128 * (i + 1)] = v[:ne]
        ref[:, 0, 128 * (i + 1) : 128 * (i + 2)] = v[ne:]

    def take(ref, i):
        return jnp.concatenate(
            [ref[:, 0, 128 * i : 128 * (i + 1)], ref[:, 0, 128 * (i + 1) : 128 * (i + 2)]], axis=0).astype(BF)

    put(s_in, 0, v_in)
    put(s_grad, 0, v_grad)

    pl.semaphore_wait(barrier, (ne - 1) + len(near))

    def to_all(i, src, dst):
        each_peer(lambda peer: pltpu.make_async_remote_copy(
            src_ref=src.at[peer], dst_ref=dst.at[e], send_sem=a2a_send.at[i], recv_sem=a2a_recv.at[i],
            device_id={"expert": peer}, device_id_type=MESH).start())
        dst[e] = src[e]

    def all_of(i, src, dst):
        return pltpu.make_async_remote_copy(
            src_ref=src.at[pl.ds(0, ne - 1)], dst_ref=dst.at[pl.ds(0, ne - 1)],
            send_sem=a2a_send.at[i], recv_sem=a2a_recv.at[i],
            device_id={"expert": lax.rem(e + 1, ne)}, device_id_type=MESH)

    to_all(0, s_in, r_in)
    to_all(3, s_grad, r_grad)

    t_f = jnp.transpose(d_f)
    t_w = jnp.transpose(d_w)
    t_hi = t_w.astype(BF)
    disp_t[0] = t_hi
    disp_t[1] = (t_w - t_hi.astype(F32)).astype(BF)
    disp_t[2] = t_f.astype(BF)
    for a in range(3):
        acc[a] = jnp.zeros(acc.shape[1:], F32)

    for c in loads[4:]:
        c.wait()
    all_of(0, s_in, r_in).wait_recv()
    xg[m, 0] = take(r_in, 0)

    def give(a, o, to):
        blk = z_at(-o)
        return pltpu.make_async_remote_copy(
            src_ref=xg.at[blk, a], dst_ref=xg.at[blk, a],
            send_sem=ag_send.at[a, to % nz], recv_sem=ag_recv.at[a, to % nz],
            device_id={"mp": z_at(to - o)}, device_id_type=MESH)

    def got(a, o):
        blk = z_at(-o)
        pltpu.make_async_remote_copy(
            src_ref=xg.at[blk, a], dst_ref=xg.at[blk, a],
            send_sem=ag_send.at[a, o % nz], recv_sem=ag_recv.at[a, o % nz],
            device_id={"mp": z_at(1)}, device_id_type=MESH).wait_recv()

    def cols(blk):
        return pl.ds(pl.multiple_of(blk * 128, 128), 128)

    def use(blk, a):
        v = xg[blk, a]
        if a == 0:
            acc[0] += dot_nt(wg[:, cols(blk)], v)
            acc[1] += dot_nt(wu[:, cols(blk)], v)
        else:
            acc[2] += dot_nt(wd[:, cols(blk)], v)

    def far(a):
        return 8 if a == 0 else -8

    def pass3(a):
        for g in (1, -1):
            got(a, 3 * g)
            for to in (6, 4, 2):
                give(a, 3 * g, to * g).start()

    def pass6(a):
        for g in (1, -1):
            got(a, 6 * g)
            if far(a) * g > 0:
                give(a, 6 * g, 8 * g).start()
            for to in (7, 5):
                give(a, 6 * g, to * g).start()

    def use_at(a, *offsets):
        for o in offsets:
            use(z_at(-o), a)

    def use_many(a, base, n):
        def body(i, carry):
            o = (1 - 2 * (i % 2)) * (base + 2 * (i // 2))
            got(a, o)
            use(z_at(-o), a)
            return carry

        lax.fori_loop(0, n, body, 0)

    for a in range(2):
        if a == 1:
            all_of(3, s_grad, r_grad).wait_recv()
            xg[m, 1] = take(r_grad, 0)
        for to in (3, -3, 1, -1):
            give(a, 0, to).start()
        use_at(a, 0)
    pass3(0)
    use_at(0, 3, -3)
    pass3(1)
    use_many(0, 1, 2)
    use_at(1, 3, -3)
    pass6(0)
    use_many(0, 2, 4)
    use_at(0, 6, -6)
    pass6(1)
    use_many(0, 5, 4)
    got(0, far(0))
    use_at(0, far(0))

    def keep(i, v):
        h_r[i] = jnp.transpose(v).astype(BF)
        h_t[i] = v.astype(BF)

    gate, up = acc[0], acc[1]
    keep(0, gate * jax.nn.sigmoid(gate) * up)

    def partial(a, blk):
        if a == 0:
            return dot(h_r[0], wd[:, cols(blk)])
        return dot(h_r[1], wg[:, cols(blk)]) + dot(h_r[2], wu[:, cols(blk)])

    def turn(a, o, to):
        return pltpu.make_async_remote_copy(
            src_ref=tx.at[a, o % nz], dst_ref=rx.at[a, o % nz],
            send_sem=rs_send.at[a, o % nz], recv_sem=rs_recv.at[a, o % nz],
            device_id={"mp": z_at(to - o)}, device_id_type=MESH)

    def came(a, o):
        turn(a, o, o + 1).wait_recv()
        return rx[a, o % nz].astype(F32)

    def weights_of(blk):
        x_v, g_v = xg[blk, 0], xg[blk, 1]
        gw_g[:, cols(blk)] = dot(h_t[1], x_v).astype(BF)
        gw_u[:, cols(blk)] = dot(h_t[2], x_v).astype(BF)
        gw_d[:, cols(blk)] = dot(h_t[0], g_v).astype(BF)

    def weights_from(first, last):
        def body(i, carry):
            weights_of(i)
            return carry

        lax.fori_loop(first, last, body, 0)

    def leaf(a, o, to):
        tx[a, o % nz] = partial(a, z_at(-o)).astype(BF)
        turn(a, o, to).start()

    def leaves(a):
        leaf(a, far(a), far(a) * 6 // 8)

        def body(i, carry):
            g = 1 - 2 * (i % 2)
            centre = 6 - 3 * (i // 4)
            o = centre - 1 + 2 * ((i // 2) % 2)
            leaf(a, g * o, g * centre)
            return carry

        lax.fori_loop(0, 8, body, 0)

    def leaves1(a):
        for g in (1, -1):
            leaf(a, g, 0)

    def part_of(a, o):
        for g in range(2):
            part[g, a] = partial(a, z_at((-o, o)[g]))

    def mid(a, o, to, kids):
        for g in range(2):
            sign = (1, -1)[g]
            total = part[g, a]
            for k in kids:
                if k < 8 or far(a) * sign > 0:
                    total = total + came(a, k * sign)
            tx[a, o * sign % nz] = total.astype(BF)
            turn(a, o * sign, to * sign).start()

    def final(a):
        total = own[a]
        for o in (1, -1, 3, -3):
            total = total + came(a, o)
        put((o_buf, b_buf)[a], 0, total)

    def give_sc(o, to):
        return pltpu.make_async_remote_copy(
            src_ref=sc_all.at[z_at(-o)], dst_ref=sc_all.at[z_at(-o)],
            send_sem=sc_send.at[to % nz], recv_sem=sc_recv.at[to % nz],
            device_id={"mp": z_at(to - o)}, device_id_type=MESH)

    def got_sc(o):
        pltpu.make_async_remote_copy(
            src_ref=sc_all.at[z_at(-o)], dst_ref=sc_all.at[z_at(-o)],
            send_sem=sc_send.at[o % nz], recv_sem=sc_recv.at[o % nz],
            device_id={"mp": z_at(1)}, device_id_type=MESH).wait_recv()

    leaves(0)
    leaves1(0)
    part_of(0, 6)

    use_many(1, 1, 2)
    use_many(1, 2, 4)
    use_at(1, 6, -6)
    mid(0, 6, 3, (5, 7, 8))
    use_many(1, 5, 4)
    got(1, far(1))
    use_at(1, far(1))
    gate, up, back = acc[0], acc[1], acc[2]
    sig = jax.nn.sigmoid(gate)
    silu = gate * sig
    keep(1, back * up * sig * (1.0 + gate * (1.0 - sig)))
    keep(2, back * silu)
    sc_all[m] = jnp.broadcast_to(jnp.sum(silu * up * back, axis=0, keepdims=True), sc_all.shape[1:])
    leaves(1)
    for to in (3, -3, 1, -1):
        give_sc(0, to).start()
    part_of(0, 3)
    part_of(1, 6)
    mid(0, 3, 0, (2, 4, 6))
    mid(1, 6, 3, (5, 7, 8))
    leaves1(1)
    for g in (1, -1):
        got_sc(3 * g)
        for to in (6, 4, 2):
            give_sc(3 * g, to * g).start()
    part_of(1, 3)
    for a in range(2):
        own[a] = partial(a, m)
    weights_from(0, 6)
    mid(1, 3, 0, (2, 4, 6))

    final(0)
    to_all(1, o_buf, o_home)
    for g in (1, -1):
        got_sc(6 * g)
        for to in (7, 5):
            give_sc(6 * g, to * g).start()
    give_sc(6, 8).start()

    for o in (1, -1, 2, -2, 4, -4, 5, -5, 7, -7, 8):
        got_sc(o)
    sc = jnp.broadcast_to(jnp.sum(sc_all[...], axis=0)[0:1, :], (ne, rows))
    row = lax.broadcasted_iota(jnp.int32, (ne, rows), 0)
    col = lax.broadcasted_iota(jnp.int32, (ne, rows), 1)
    sc_col = [jnp.sum(jnp.where(col == row + ne * i, sc, 0.0), axis=1, keepdims=True) for i in range(2)]
    lane = lax.broadcasted_iota(jnp.int32, (ne, 128), 1)
    b_buf[:, 0, 256:384] = jnp.where(lane == 0, sc_col[0], jnp.where(lane == 1, sc_col[1], 0.0))

    final(1)
    to_all(2, b_buf, b_home)
    weights_from(6, 16)

    all_of(1, o_buf, o_home).wait_recv()
    out = take(o_home, 0)
    mixed[...] = (dot(disp_t[0], out) + dot(disp_t[1], out)).astype(BF)

    for i, refs in enumerate(
        ((s_in, r_in), (o_buf, o_home), (b_buf, b_home), (s_grad, r_grad))
    ):
        all_of(i, *refs).wait_send()
    for o in range(1, nz):
        for a in range(2):
            give(a, 0, o).wait_send()
            turn(a, o, 0).wait_send()
        give_sc(0, o).wait_send()
    all_of(2, b_buf, b_home).wait_recv()

    gtok[...] = dot(disp_t[2], take(b_home, 0)).astype(BF)
    score = b_home[:, 0, 256:384]
    score = disp[...] * jnp.concatenate([score[:, 0:1], score[:, 1:2]], axis=0)
    for k in range(topk):
        picked = jnp.sum(jnp.where(rt[k : k + 1, :] == e_r, score, 0.0), axis=0, keepdims=True)
        gprob[k : k + 1, :] = picked / pt[k : k + 1, :]


def write_out(*refs):
    n = len(refs) // 2
    sems = refs[-1]
    copies = [pltpu.make_async_copy(refs[i], refs[n + i], sems.at[i]) for i in range(n)]
    for c in copies:
        c.start()
    for c in copies:
        c.wait()


def local(ne, nz, tokens, routes, probs, w_gate, w_up, w_down, grad_out):
    nt, width = tokens.shape
    topk = routes.shape[1]
    d, f = w_gate.shape[1:]
    rows = ne * 2
    vmem = pl.BlockSpec(memory_space=pltpu.VMEM)
    hbm = pl.BlockSpec(memory_space=pl.ANY)
    dma = pltpu.SemaphoreType.DMA
    V = pltpu.VMEM
    shapes = (
        jax.ShapeDtypeStruct((nt, width), BF),
        jax.ShapeDtypeStruct((nt, width), BF),
        jax.ShapeDtypeStruct((topk, nt), F32),
        jax.ShapeDtypeStruct((f, d), BF),
        jax.ShapeDtypeStruct((f, d), BF),
        jax.ShapeDtypeStruct((f, d), BF),
    )
    outs = pl.pallas_call(
        functools.partial(kernel, ne, nz),
        out_shape=tuple(pltpu.VMEM(t.shape, t.dtype) for t in shapes),
        in_specs=[hbm] * 7,
        out_specs=(vmem,) * 6,
        scratch_shapes=[
            V((nt, width), BF), V((nt, width), BF), V((topk, nt), jnp.int32), V((topk, nt), F32),
            V((f, d), BF), V((f, d), BF), V((f, d), BF),
            V((rows, nt), F32), V((3, nt, rows), BF),
            V((ne, 1, 256), F32), V((ne, 1, 256), F32), V((ne, 1, 256), F32), V((ne, 1, 256), F32),
            V((nz, 2, rows, width), BF),
            V((3, f, rows), F32), V((3, f, rows), BF), V((3, rows, f), BF),
            V((2, 2, rows, width), F32),
            V((2, nz, rows, width), BF), V((2, nz, rows, width), BF),
            V((2, rows, width), F32),
            V((nz, 8, rows), F32),
            V((ne, 1, 256), F32), V((ne, 1, 256), F32), V((ne, 1, 384), F32), V((ne, 1, 384), F32),
            dma((7,)), dma((4,)), dma((4,)),
            dma((2, nz)), dma((2, nz)), dma((2, nz)), dma((2, nz)),
            dma((nz,)), dma((nz,)),
        ],
        compiler_params=pltpu.CompilerParams(
            collective_id=0, has_side_effects=True, vmem_limit_bytes=65700000
        ),
    )(
        tokens, grad_out, routes.T, probs.T,
        jnp.swapaxes(w_gate, 1, 2).reshape(f, d), jnp.swapaxes(w_up, 1, 2).reshape(f, d), w_down.reshape(f, d),
    )
    outs = pl.pallas_call(
        write_out,
        out_shape=shapes,
        in_specs=[hbm] * 6,
        out_specs=(pl.BlockSpec(memory_space=pltpu.HBM),) * 6,
        scratch_shapes=[dma((6,))],
        compiler_params=pltpu.CompilerParams(vmem_limit_bytes=1024 * 1024),
    )(*outs)
    mixed, gtok, gprob, gg, gu, gd = outs
    return (
        mixed, gtok, gprob.T,
        jnp.swapaxes(gg.reshape(1, f, d), 1, 2), jnp.swapaxes(gu.reshape(1, f, d), 1, 2), gd.reshape(1, f, d),
    )


def solution(mesh):
    ne, nz = mesh.shape["expert"], mesh.shape["mp"]
    placed = (
        P("expert", "mp"),
        P("expert", None),
        P("expert", None),
        P("expert", None, "mp"),
        P("expert", None, "mp"),
        P("expert", "mp", None),
        P("expert", "mp"),
    )
    return jax.shard_map(
        functools.partial(local, ne, nz),
        mesh=mesh,
        in_specs=placed,
        out_specs=(
            P("expert", "mp"),
            P("expert", "mp"),
            P("expert", None),
            P("expert", None, "mp"),
            P("expert", None, "mp"),
            P("expert", "mp", None),
        ),
        check_vma=False,
    )
```
